32 devices in a mesh: walk: 16 (over z, x, core), elec: 2 (over y).
Axes of the slice: x: 2, y: 2, z: 4, core: 2. Of those that a mesh axis runs over, the one named last changes fastest.
Arguments:
- positions: float32 [96, 3, 200], P('walk', None, 'elec'), may hold values from -5 to 5
- targets: bfloat16 [96, 200, 3200], P('walk', 'elec'), may hold values from -6 to 6
- w_in: float32 [4, 256], replicated, may hold values from -3 to 3
- v_in: float32 [4, 32], replicated, may hold values from -3 to 3
- w_up: float32 [2, 256, 32], replicated, may hold values from -0.375 to 0.375
- w_gate: float32 [2, 32, 32], replicated, may hold values from -1 to 1
- w_mix: float32 [2, 256, 256], replicated, may hold values from -0.375 to 0.375
- w_msg: float32 [2, 32, 256], replicated, may hold values from -1 to 1
- bias: float32 [2, 256], replicated, may hold values from -3 to 3
- w_head: bfloat16 [256, 3200], replicated, may hold values from -0.375 to 0.375
Outputs:
- grad_head: float32 [3200, 256], P('walk')
- grad_in: float32 [4, 256], replicated
- grad_up: float32 [2, 256, 32], replicated
- grad_gate: float32 [2, 32, 32], replicated
- grad_mix: float32 [2, 256, 256], replicated
- grad_msg: float32 [2, 32, 256], replicated
- grad_bias: float32 [2, 256], replicated
The draws below stay inside these ranges and needn't reach their ends.
All inputs are finite; a program needn't handle non-finite values.
Results may differ from the reference program's by a relative error of at most 0.0003.
Values sent between devices are 32-bit elements; how exact they have to be, the bound alone decides.
A program may use at most 192 MiB of HBM per device.

```python
import jax
import jax.numpy as jnp
from jax import lax

E = 200
H = 256
P_SIZE = 32
LAYERS = 2
W_DEV = 6
K = 3200
WALKERS = 96


def steps_of(key, extent, cuts, smallest, high):
    factor_of = 1.0
    for dim, parts in cuts:
        steps = jax.random.uniform(jax.random.fold_in(jax.random.fold_in(key, 6), dim), (parts,), jnp.float32, smallest / len(cuts), high / len(cuts))
        factor_of = factor_of * jnp.repeat(jnp.exp(steps), extent[dim] // parts).reshape((-1,) + (1,) * (len(extent) - 1 - dim))
    return factor_of


def noise(stream_key, extent, deviation, limit, shards=(), dtype=jnp.bfloat16):
    level = steps_of(stream_key, extent, shards, -0.22, 0.18) if shards else 1.0
    array = jax.random.normal(stream_key, extent, jnp.float32) * deviation * level
    return jnp.minimum(jnp.maximum(array, -limit), limit).astype(dtype)


def setup_inputs(seed: int = 0) -> dict:
    streams_of = jax.random.split(jax.random.key(seed), 11)
    return {
        "positions": noise(streams_of[0], (WALKERS, 3, E), 1.0, 5.0, ((0, 16), (2, 2)), jnp.float32),
        "targets": noise(streams_of[1], (WALKERS, E, K), 1.0, 6.0, ((0, 16), (1, 2))),
        "w_in": noise(streams_of[2], (4, H), 4 ** -0.5, 3.0, (), jnp.float32),
        "v_in": noise(streams_of[3], (4, P_SIZE), 4 ** -0.5, 3.0, (), jnp.float32),
        "w_up": noise(streams_of[4], (LAYERS, H, P_SIZE), H ** -0.5, 0.375, (), jnp.float32),
        "w_gate": noise(streams_of[5], (LAYERS, P_SIZE, P_SIZE), P_SIZE ** -0.5, 1.0, (), jnp.float32),
        "w_mix": noise(streams_of[6], (LAYERS, H, H), H ** -0.5, 0.375, (), jnp.float32),
        "w_msg": noise(streams_of[7], (LAYERS, P_SIZE, H), P_SIZE ** -0.5, 1.0, (), jnp.float32),
        "bias": noise(streams_of[8], (LAYERS, H), 0.5, 3.0, (), jnp.float32),
        "w_head": noise(streams_of[9], (H, K), H ** -0.5, 0.375),
    }


HI = lax.Precision.HIGHEST

def embed_states(pos_rows, w_in):
    radius = jnp.sqrt(lax.optimization_barrier(jnp.sum(pos_rows * pos_rows, axis=1)) + 1.0)
    feats = jnp.concatenate([pos_rows, radius[:, None, :]], axis=1)
    return jnp.tanh(jnp.einsum('wci,ch->wih', feats, w_in, precision=HI))

def embed_pairs(pos_rows, pos_all, v_in):
    diff = pos_rows[:, :, :, None] - pos_all[:, :, None, :]
    dist = jnp.sqrt(lax.optimization_barrier(jnp.sum(diff * diff, axis=1)) + 1.0)
    feats = jnp.concatenate([diff, dist[:, None]], axis=1)
    return jnp.tanh(jnp.einsum('wcie,cp->wiep', feats, v_in, precision=HI))

def layer_update(h_rows, s_all, pairs, w_mix, w_msg, bias, w_gate):
    gates = jax.nn.sigmoid(jnp.einsum('wiep,pq->wieq', pairs, w_gate, precision=HI))
    message = jnp.einsum('wieq,weq->wiq', gates, s_all, precision=HI) / s_all.shape[1]
    pre = jnp.einsum('wih,hk->wik', h_rows, w_mix, precision=HI)
    pre = pre + jnp.einsum('wiq,qk->wik', message, w_msg, precision=HI) + bias
    return jnp.tanh(pre) + h_rows

def reference(positions, targets, w_in, v_in, w_up, w_gate, w_mix, w_msg, bias, w_head):
    walkers = positions.shape[0]
    blocks = walkers // W_DEV
    pos_b = positions.reshape(blocks, W_DEV, 3, E)
    tgt_b = targets.reshape(blocks, W_DEV * E, K)
    params = (w_in, w_up, w_gate, w_mix, w_msg, bias)

    def trunk(prm, pos, pairs):
        p_in, p_up, p_gate, p_mix, p_msg, p_bias = prm
        states = embed_states(pos, p_in)
        for layer in range(LAYERS):
            proj = jnp.einsum('wjh,hp->wjp', states, p_up[layer], precision=HI)
            states = layer_update(states, proj, pairs, p_mix[layer], p_msg[layer], p_bias[layer], p_gate[layer])
        return states

    def step(carry, xs):
        pos, tgt = xs
        pairs = embed_pairs(pos, pos, v_in)
        final, pull = jax.vjp(lambda prm: trunk(prm, pos, pairs), params)
        last = final.reshape(-1, H).astype(jnp.bfloat16)
        orbitals = jnp.dot(last, w_head, preferred_element_type=jnp.float32)
        d_orb = (2.0 / walkers * (orbitals - tgt.astype(jnp.float32))).astype(jnp.bfloat16)
        head = lax.dot_general(d_orb, last, (((0,), (0,)), ((), ())), preferred_element_type=jnp.float32)
        d_last = lax.dot_general(d_orb, w_head, (((1,), (1,)), ((), ())), preferred_element_type=jnp.float32)
        grads = pull(d_last.reshape(final.shape))[0]
        total_head, totals = carry
        return ((total_head + head, tuple((a + b for a, b in zip(totals, grads)))), None)
    init = (jnp.zeros((K, H), jnp.float32), tuple((jnp.zeros(p.shape, jnp.float32) for p in params)))
    (grad_head, grads), _ = lax.scan(step, init, (pos_b, tgt_b))
    return (grad_head, grads[0], grads[1], grads[2], grads[3], grads[4], grads[5])
```

```python
import functools

import jax
import jax.numpy as jnp
from jax import lax
from jax.experimental import pallas as pl
from jax.experimental.pallas import tpu as pltpu
from jax.sharding import PartitionSpec as P

LAYERS = 2
PACK = 8
CHUNK = 5

HI = lax.Precision.HIGHEST
F32 = jnp.float32
BF16 = jnp.bfloat16


def split(x):
    high = x.astype(BF16)
    return high, (x - high.astype(F32)).astype(BF16)


def pair_kernel(groups, rows, xi_ref, xj_ref, v_ref, w_ref, proj_ref, fold_ref, pairs_ref, t0_ref, t1_ref, msg_ref):
    width = v_ref.shape[1]
    w_high, w_low = split(w_ref[...])
    acc = jnp.zeros((rows, width), F32)
    total = jnp.zeros((1, width), F32)
    for start in range(0, groups, CHUNK):
        for k in range(start, start + CHUNK):
            dx = xi_ref[0, :, 0:1] - xj_ref[0, k, 0:1, :]
            dy = xi_ref[0, :, 1:2] - xj_ref[0, k, 1:2, :]
            dz = xi_ref[0, :, 2:3] - xj_ref[0, k, 2:3, :]
            dist = jnp.sqrt(dx * dx + dy * dy + dz * dz + 1.0)
            pre = dx * v_ref[0:1, :] + dy * v_ref[1:2, :] + dz * v_ref[2:3, :] + dist * v_ref[3:4, :]
            pairs_ref[0, k] = jnp.tanh(pre)
        flat = pairs_ref[0, start : start + CHUNK].reshape(CHUNK * rows, width)
        high, low = split(flat)
        z = jnp.dot(high, w_high, preferred_element_type=F32)
        z = z + jnp.dot(low, w_high, preferred_element_type=F32)
        z = z + jnp.dot(high, w_low, preferred_element_type=F32)
        t = jnp.tanh(z)
        t0_ref[0, start : start + CHUNK] = t[:, :width].reshape(CHUNK, rows, width)
        t1_ref[0, start : start + CHUNK] = t[:, width:].reshape(CHUNK, rows, width)
        for k in range(start, start + CHUNK):
            row = proj_ref[0, k]
            acc = acc + t0_ref[0, k] * row
            total = total + row
    msg_ref[0] = jnp.dot(acc + total, fold_ref[...], precision=HI, preferred_element_type=F32)


def message_kernel(groups, rows, t_ref, proj_ref, fold_ref, msg_ref):
    width = t_ref.shape[3]
    acc = jnp.zeros((rows, width), F32)
    total = jnp.zeros((1, width), F32)
    for k in range(groups):
        row = proj_ref[0, k]
        acc = acc + t_ref[0, k] * row
        total = total + row
    msg_ref[0] = jnp.dot(acc + total, fold_ref[...], precision=HI, preferred_element_type=F32)


def back_kernel(groups, rows, pairs_ref, t_ref, proj_ref, dm_ref, dproj_ref, gate_ref, tiled_ref, dz_ref):
    width = t_ref.shape[3]

    @pl.when(pl.program_id(0) == 0)
    def _():
        gate_ref[...] = jnp.zeros_like(gate_ref)

    tiled_ref[...] = jnp.concatenate([dm_ref[0]] * PACK, axis=1)
    dims = (((0,), (0,)), ((), ()))
    for start in range(0, groups, CHUNK):
        for k in range(start, start + CHUNK):
            t = t_ref[0, k]
            both = tiled_ref[...] * (1.0 + t)
            dproj_ref[0, k] = jnp.sum(both, axis=0, keepdims=True)
            dz_ref[k - start] = both * (1.0 - t) * proj_ref[0, k]
        p_high, p_low = split(pairs_ref[0, start : start + CHUNK].reshape(CHUNK * rows, width))
        d_high, d_low = split(dz_ref[...].reshape(CHUNK * rows, width))
        part = lax.dot_general(p_high, d_high, dims, preferred_element_type=F32)
        part = part + lax.dot_general(p_low, d_high, dims, preferred_element_type=F32)
        part = part + lax.dot_general(p_high, d_low, dims, preferred_element_type=F32)
        gate_ref[...] += part


def whole(shape):
    return pl.BlockSpec(shape, lambda w: (0,) * len(shape))


def per_walker(shape):
    return pl.BlockSpec((1,) + shape, lambda w: (w,) + (0,) * len(shape))


PARAMS = pltpu.CompilerParams(vmem_limit_bytes=50 * 1024 * 1024)


def on_device(positions, targets, w_in, v_in, w_up, w_gate, w_mix, w_msg, bias, w_head):
    walk_size = lax.axis_size("walk")
    elec_size = lax.axis_size("elec")
    own, _, mine = positions.shape
    walkers = own * walk_size
    every = mine * elec_size
    features = v_in.shape[1]
    width = PACK * features
    groups = every // PACK
    rows = -(-mine // 8) * 8

    pos_all = lax.all_gather(positions, "elec", axis=2, tiled=True)
    me = lax.axis_index("elec")

    feats = jnp.concatenate(
        [pos_all, jnp.sqrt(jnp.sum(pos_all * pos_all, axis=1, keepdims=True) + 1.0)], axis=1
    )
    states_all = jnp.tanh(jnp.einsum("wci,ch->wih", feats, w_in, precision=HI))
    proj = jnp.einsum("wjh,hp->wjp", states_all, w_up[0], precision=HI)
    own_feats = lax.dynamic_slice_in_dim(feats, me * mine, mine, 2)
    states0 = lax.dynamic_slice_in_dim(states_all, me * mine, mine, 1)

    xi = jnp.pad(jnp.transpose(positions, (0, 2, 1)), ((0, 0), (0, rows - mine), (0, 0)))
    xj = jnp.transpose(pos_all.reshape(own, 3, groups, PACK), (0, 2, 1, 3))
    xj = jnp.repeat(xj, features, axis=3)
    v_tiled = jnp.tile(v_in, (1, PACK))
    eye = jnp.eye(PACK, dtype=F32)
    blocks = [
        (0.5 * eye[:, None, :, None] * w_gate[l][None, :, None, :]).reshape(width, width)
        for l in range(LAYERS)
    ]
    w_pair = jnp.concatenate(blocks, axis=1)
    fold = jnp.tile(jnp.eye(features, dtype=F32), (PACK, 1)) * (0.5 / every)

    big = jax.ShapeDtypeStruct((own, groups, rows, width), F32)
    small = jax.ShapeDtypeStruct((own, rows, features), F32)
    big_spec = per_walker((groups, rows, width))
    row_spec = per_walker((groups, 1, width))
    small_spec = per_walker((rows, features))

    def as_rows(p):
        return p.reshape(own, groups, 1, width)

    rows0 = as_rows(proj)
    pairs, t0, t1, msg = pl.pallas_call(
        functools.partial(pair_kernel, groups, rows),
        grid=(own,),
        out_shape=(big, big, big, small),
        in_specs=[
            per_walker((rows, 3)),
            per_walker((groups, 3, width)),
            whole((4, width)),
            whole((width, LAYERS * width)),
            row_spec,
            whole((width, features)),
        ],
        out_specs=(big_spec, big_spec, big_spec, small_spec),
        compiler_params=PARAMS,
    )(xi, xj, v_tiled, w_pair, rows0, fold)

    def update(h, message, layer):
        pre = jnp.einsum("wih,hk->wik", h, w_mix[layer], precision=HI)
        pre = pre + jnp.einsum("wiq,qk->wik", message, w_msg[layer], precision=HI) + bias[layer]
        return jnp.tanh(pre)

    msg0 = msg[:, :mine]
    act0 = update(states0, msg0, 0)
    states1 = act0 + states0
    local_proj = jnp.einsum("wjh,hp->wjp", states1, w_up[1], precision=HI)
    rows1 = as_rows(lax.all_gather(local_proj, "elec", axis=1, tiled=True))
    msg = pl.pallas_call(
        functools.partial(message_kernel, groups, rows),
        grid=(own,),
        out_shape=small,
        in_specs=[big_spec, row_spec, whole((width, features))],
        out_specs=small_spec,
        compiler_params=PARAMS,
    )(t1, rows1, fold)
    msg1 = msg[:, :mine]
    act1 = update(states1, msg1, 1)
    states2 = act1 + states1

    last = states2.reshape(-1, states2.shape[2]).astype(BF16)
    orbitals = jnp.dot(last, w_head, preferred_element_type=F32)
    flat_targets = targets.reshape(-1, targets.shape[2]).astype(F32)
    d_orb = (2.0 / walkers * (orbitals - flat_targets)).astype(BF16)
    d_states = lax.dot_general(d_orb, w_head, (((1,), (1,)), ((), ())), preferred_element_type=F32)
    d_states = d_states.reshape(states2.shape)
    head = lax.dot_general(d_orb, last, (((0,), (0,)), ((), ())), preferred_element_type=F32)
    head_part = lax.psum_scatter(head, "walk", scatter_dimension=0, tiled=True)

    def back(d_out, h, act, message, t, rows_l, layer):
        d_pre = d_out * (1.0 - act * act)
        g_bias = jnp.sum(d_pre, axis=(0, 1))
        g_mix = jnp.einsum("wih,wik->hk", h, d_pre, precision=HI)
        g_msg = jnp.einsum("wiq,wik->qk", message, d_pre, precision=HI)
        d_msg = jnp.einsum("wik,qk->wiq", d_pre, w_msg[layer], precision=HI) * (0.5 / every)
        d_msg = jnp.pad(d_msg, ((0, 0), (0, rows - mine), (0, 0)))
        d_rows, g_wide = pl.pallas_call(
            functools.partial(back_kernel, groups, rows),
            grid=(own,),
            out_shape=(
                jax.ShapeDtypeStruct((own, groups, 1, width), F32),
                jax.ShapeDtypeStruct((width, width), F32),
            ),
            in_specs=[big_spec, big_spec, row_spec, small_spec],
            out_specs=(row_spec, whole((width, width))),
            scratch_shapes=[pltpu.VMEM((rows, width), F32), pltpu.VMEM((CHUNK, rows, width), F32)],
            compiler_params=PARAMS,
        )(pairs, t, rows_l, d_msg)
        g_gate = 0.5 * sum(
            g_wide[k * features : (k + 1) * features, k * features : (k + 1) * features]
            for k in range(PACK)
        )
        d_proj = d_rows.reshape(own, every, features)
        d_own = lax.psum_scatter(d_proj, "elec", scatter_dimension=1, tiled=True)
        g_up = jnp.einsum("wjh,wjp->hp", h, d_own, precision=HI)
        d_in = d_out + jnp.einsum("wik,hk->wih", d_pre, w_mix[layer], precision=HI)
        d_in = d_in + jnp.einsum("wjp,hp->wjh", d_own, w_up[layer], precision=HI)
        return d_in, g_up, g_gate, g_mix, g_msg, g_bias

    d1, *g1 = back(d_states, states1, act1, msg1, t1, rows1, 1)
    d0, *g0 = back(d1, states0, act0, msg0, t0, rows0, 0)
    g_in = jnp.einsum("wci,wih->ch", own_feats, d0 * (1.0 - states0 * states0), precision=HI)
    return finish(head_part, g_in, *[jnp.stack([a, b]) for a, b in zip(g0, g1)])


def finish(head_part, *grads):
    return (lax.psum(head_part, "elec"),) + lax.psum(grads, ("walk", "elec"))


def solution(mesh):
    return jax.shard_map(
        on_device,
        mesh=mesh,
        in_specs=(P("walk", None, "elec"), P("walk", "elec", None)) + (P(),) * 8,
        out_specs=(P("walk", None),) + (P(),) * 6,
        check_vma=False,
    )
```

```python
import functools

import jax
import jax.numpy as jnp
from jax import lax
from jax.experimental import pallas as pl
from jax.experimental.pallas import tpu as pltpu
from jax.sharding import PartitionSpec as P

LAYERS = 2
PACK = 8
CHUNK = 5

HI = lax.Precision.HIGHEST
F32 = jnp.float32
BF16 = jnp.bfloat16


def split(x):
    high = x.astype(BF16)
    return high, (x - high.astype(F32)).astype(BF16)


def pair_kernel(groups, rows, xi_ref, xj_ref, v_ref, w_ref, proj_ref, fold_ref, pairs_ref, t0_ref, t1_ref, msg_ref):
    width = v_ref.shape[1]
    w_high, w_low = split(w_ref[...])
    acc = jnp.zeros((rows, width), F32)
    total = jnp.zeros((1, width), F32)
    for start in range(0, groups, CHUNK):
        for k in range(start, start + CHUNK):
            dx = xi_ref[0, :, 0:1] - xj_ref[0, k, 0:1, :]
            dy = xi_ref[0, :, 1:2] - xj_ref[0, k, 1:2, :]
            dz = xi_ref[0, :, 2:3] - xj_ref[0, k, 2:3, :]
            dist = jnp.sqrt(dx * dx + dy * dy + dz * dz + 1.0)
            pre = dx * v_ref[0:1, :] + dy * v_ref[1:2, :] + dz * v_ref[2:3, :] + dist * v_ref[3:4, :]
            pairs_ref[0, k] = jnp.tanh(pre)
        flat = pairs_ref[0, start : start + CHUNK].reshape(CHUNK * rows, width)
        high, low = split(flat)
        z = jnp.dot(high, w_high, preferred_element_type=F32)
        z = z + jnp.dot(low, w_high, preferred_element_type=F32)
        z = z + jnp.dot(high, w_low, preferred_element_type=F32)
        t = jnp.tanh(z)
        t0_ref[0, start : start + CHUNK] = t[:, :width].reshape(CHUNK, rows, width)
        t1_ref[0, start : start + CHUNK] = t[:, width:].reshape(CHUNK, rows, width)
        for k in range(start, start + CHUNK):
            row = proj_ref[0, k]
            acc = acc + t0_ref[0, k] * row
            total = total + row
    msg_ref[0] = jnp.dot(acc + total, fold_ref[...], precision=HI, preferred_element_type=F32)


def message_kernel(groups, rows, t_ref, proj_ref, fold_ref, msg_ref):
    width = t_ref.shape[3]
    acc = jnp.zeros((rows, width), F32)
    total = jnp.zeros((1, width), F32)
    for k in range(groups):
        row = proj_ref[0, k]
        acc = acc + t_ref[0, k] * row
        total = total + row
    msg_ref[0] = jnp.dot(acc + total, fold_ref[...], precision=HI, preferred_element_type=F32)


def back_kernel(groups, rows, pairs_ref, t_ref, proj_ref, dm_ref, dproj_ref, gate_ref, tiled_ref, dz_ref):
    width = t_ref.shape[3]

    @pl.when(pl.program_id(0) == 0)
    def _():
        gate_ref[...] = jnp.zeros_like(gate_ref)

    tiled_ref[...] = jnp.concatenate([dm_ref[0]] * PACK, axis=1)
    dims = (((0,), (0,)), ((), ()))
    for start in range(0, groups, CHUNK):
        for k in range(start, start + CHUNK):
            t = t_ref[0, k]
            both = tiled_ref[...] * (1.0 + t)
            dproj_ref[0, k] = jnp.sum(both, axis=0, keepdims=True)
            dz_ref[k - start] = both * (1.0 - t) * proj_ref[0, k]
        p_high, p_low = split(pairs_ref[0, start : start + CHUNK].reshape(CHUNK * rows, width))
        d_high, d_low = split(dz_ref[...].reshape(CHUNK * rows, width))
        part = lax.dot_general(p_high, d_high, dims, preferred_element_type=F32)
        part = part + lax.dot_general(p_low, d_high, dims, preferred_element_type=F32)
        part = part + lax.dot_general(p_high, d_low, dims, preferred_element_type=F32)
        gate_ref[...] += part


def swap(x, axis, bit):
    size = lax.axis_size(axis)
    return lax.ppermute(x, axis, [(i, i ^ bit) for i in range(size)])


def bits_of(axis):
    return [1 << k for k in range(lax.axis_size(axis).bit_length() - 1)]


def sum_over(x, axis):
    for bit in bits_of(axis):
        x = x + swap(x, axis, bit)
    return x


def sum_scatter(x, axis):
    me = lax.axis_index(axis)
    for bit in bits_of(axis):
        mine = (me // bit) % 2
        x = x.reshape((x.shape[0] // 2, 2) + x.shape[1:])
        keep = lax.dynamic_index_in_dim(x, mine, 1, keepdims=False)
        send = lax.dynamic_index_in_dim(x, 1 - mine, 1, keepdims=False)
        x = keep + swap(send, axis, bit)
    return x


def gather(x, axis):
    me = lax.axis_index(axis)
    for bit in reversed(bits_of(axis)):
        first = (me // bit) % 2 == 0
        other = swap(x, axis, bit)
        pair = jnp.stack([jnp.where(first, x, other), jnp.where(first, other, x)], axis=1)
        x = pair.reshape((pair.shape[0] * 2,) + x.shape[1:])
    return x


def whole(shape):
    return pl.BlockSpec(shape, lambda w: (0,) * len(shape))


def per_walker(shape):
    return pl.BlockSpec((1,) + shape, lambda w: (w,) + (0,) * len(shape))


PARAMS = pltpu.CompilerParams(vmem_limit_bytes=50 * 1024 * 1024)


def on_device(positions, targets, w_in, v_in, w_up, w_gate, w_mix, w_msg, bias, w_head):
    walk_size = lax.axis_size("walk")
    elec_size = lax.axis_size("elec")
    own, _, mine = positions.shape
    walkers = own * walk_size
    every = mine * elec_size
    features = v_in.shape[1]
    width = PACK * features
    groups = every // PACK
    rows = -(-mine // 8) * 8

    pos_all = jnp.moveaxis(gather(positions[None], "elec"), 0, 2).reshape(own, 3, every)
    me = lax.axis_index("elec")

    feats = jnp.concatenate(
        [pos_all, jnp.sqrt(jnp.sum(pos_all * pos_all, axis=1, keepdims=True) + 1.0)], axis=1
    )
    states_all = jnp.tanh(jnp.einsum("wci,ch->wih", feats, w_in, precision=HI))
    proj = jnp.einsum("wjh,hp->wjp", states_all, w_up[0], precision=HI)
    own_feats = lax.dynamic_slice_in_dim(feats, me * mine, mine, 2)
    states0 = lax.dynamic_slice_in_dim(states_all, me * mine, mine, 1)

    xi = jnp.pad(jnp.transpose(positions, (0, 2, 1)), ((0, 0), (0, rows - mine), (0, 0)))
    xj = jnp.transpose(pos_all.reshape(own, 3, groups, PACK), (0, 2, 1, 3))
    xj = jnp.repeat(xj, features, axis=3)
    v_tiled = jnp.tile(v_in, (1, PACK))
    eye = jnp.eye(PACK, dtype=F32)
    blocks = [
        (0.5 * eye[:, None, :, None] * w_gate[l][None, :, None, :]).reshape(width, width)
        for l in range(LAYERS)
    ]
    w_pair = jnp.concatenate(blocks, axis=1)
    fold = jnp.tile(jnp.eye(features, dtype=F32), (PACK, 1)) * (0.5 / every)

    big = jax.ShapeDtypeStruct((own, groups, rows, width), F32)
    small = jax.ShapeDtypeStruct((own, rows, features), F32)
    big_spec = per_walker((groups, rows, width))
    row_spec = per_walker((groups, 1, width))
    small_spec = per_walker((rows, features))

    def as_rows(p):
        return p.reshape(own, groups, 1, width)

    rows0 = as_rows(proj)
    pairs, t0, t1, msg = pl.pallas_call(
        functools.partial(pair_kernel, groups, rows),
        grid=(own,),
        out_shape=(big, big, big, small),
        in_specs=[
            per_walker((rows, 3)),
            per_walker((groups, 3, width)),
            whole((4, width)),
            whole((width, LAYERS * width)),
            row_spec,
            whole((width, features)),
        ],
        out_specs=(big_spec, big_spec, big_spec, small_spec),
        compiler_params=PARAMS,
    )(xi, xj, v_tiled, w_pair, rows0, fold)

    def update(h, message, layer):
        pre = jnp.einsum("wih,hk->wik", h, w_mix[layer], precision=HI)
        pre = pre + jnp.einsum("wiq,qk->wik", message, w_msg[layer], precision=HI) + bias[layer]
        return jnp.tanh(pre)

    msg0 = msg[:, :mine]
    act0 = update(states0, msg0, 0)
    states1 = act0 + states0
    local_proj = jnp.einsum("wjh,hp->wjp", states1, w_up[1], precision=HI)
    rows1 = as_rows(jnp.moveaxis(gather(local_proj[None], "elec"), 0, 1))
    msg = pl.pallas_call(
        functools.partial(message_kernel, groups, rows),
        grid=(own,),
        out_shape=small,
        in_specs=[big_spec, row_spec, whole((width, features))],
        out_specs=small_spec,
        compiler_params=PARAMS,
    )(t1, rows1, fold)
    msg1 = msg[:, :mine]
    act1 = update(states1, msg1, 1)
    states2 = act1 + states1

    last = states2.reshape(-1, states2.shape[2]).astype(BF16)
    orbitals = jnp.dot(last, w_head, preferred_element_type=F32)
    flat_targets = targets.reshape(-1, targets.shape[2]).astype(F32)
    d_orb = (2.0 / walkers * (orbitals - flat_targets)).astype(BF16)
    d_states = lax.dot_general(d_orb, w_head, (((1,), (1,)), ((), ())), preferred_element_type=F32)
    d_states = d_states.reshape(states2.shape)
    head = lax.dot_general(d_orb, last, (((0,), (0,)), ((), ())), preferred_element_type=F32)
    head_part = lax.psum_scatter(head, "walk", scatter_dimension=0, tiled=True)

    def back(d_out, h, act, message, t, rows_l, layer):
        d_pre = d_out * (1.0 - act * act)
        g_bias = jnp.sum(d_pre, axis=(0, 1))
        g_mix = jnp.einsum("wih,wik->hk", h, d_pre, precision=HI)
        g_msg = jnp.einsum("wiq,wik->qk", message, d_pre, precision=HI)
        d_msg = jnp.einsum("wik,qk->wiq", d_pre, w_msg[layer], precision=HI) * (0.5 / every)
        d_msg = jnp.pad(d_msg, ((0, 0), (0, rows - mine), (0, 0)))
        d_rows, g_wide = pl.pallas_call(
            functools.partial(back_kernel, groups, rows),
            grid=(own,),
            out_shape=(
                jax.ShapeDtypeStruct((own, groups, 1, width), F32),
                jax.ShapeDtypeStruct((width, width), F32),
            ),
            in_specs=[big_spec, big_spec, row_spec, small_spec],
            out_specs=(row_spec, whole((width, width))),
            scratch_shapes=[pltpu.VMEM((rows, width), F32), pltpu.VMEM((CHUNK, rows, width), F32)],
            compiler_params=PARAMS,
        )(pairs, t, rows_l, d_msg)
        g_gate = 0.5 * sum(
            g_wide[k * features : (k + 1) * features, k * features : (k + 1) * features]
            for k in range(PACK)
        )
        d_proj = d_rows.reshape(own, elec_size, mine, features)
        d_own = sum_scatter(jnp.moveaxis(d_proj, 1, 0), "elec")[0]
        g_up = jnp.einsum("wjh,wjp->hp", h, d_own, precision=HI)
        d_in = d_out + jnp.einsum("wik,hk->wih", d_pre, w_mix[layer], precision=HI)
        d_in = d_in + jnp.einsum("wjp,hp->wjh", d_own, w_up[layer], precision=HI)
        return d_in, g_up, g_gate, g_mix, g_msg, g_bias

    d1, *g1 = back(d_states, states1, act1, msg1, t1, rows1, 1)
    d0, *g0 = back(d1, states0, act0, msg0, t0, rows0, 0)
    g_in = jnp.einsum("wci,wih->ch", own_feats, d0 * (1.0 - states0 * states0), precision=HI)
    return finish(head_part, g_in, *[jnp.stack([a, b]) for a, b in zip(g0, g1)])


def finish(head_part, *grads):
    size = lax.axis_size("walk")
    width = grads[0].shape[-1]
    flat = jnp.concatenate([g.reshape(-1, width) for g in grads])
    count = flat.shape[0]
    block = -(-count // (8 * size)) * 8
    flat = jnp.pad(flat, ((0, block * size - count), (0, 0))).reshape(size, block, width)
    flat = gather(sum_over(sum_scatter(flat, "walk"), "elec"), "walk").reshape(-1, width)
    outs = []
    start = 0
    for g in grads:
        rows = g.size // width
        outs.append(flat[start : start + rows].reshape(g.shape))
        start += rows
    return (sum_over(head_part, "elec"),) + tuple(outs)


def solution(mesh):
    return jax.shard_map(
        on_device,
        mesh=mesh,
        in_specs=(P("walk", None, "elec"), P("walk", "elec", None)) + (P(),) * 8,
        out_specs=(P("walk", None),) + (P(),) * 6,
        check_vma=False,
    )
```

```python
import functools

import jax
import jax.numpy as jnp
from jax import lax
from jax.experimental import pallas as pl
from jax.experimental.pallas import tpu as pltpu
from jax.sharding import PartitionSpec as P

LAYERS = 2
PACK = 8
CHUNK = 5

HI = lax.Precision.HIGHEST
F32 = jnp.float32
BF16 = jnp.bfloat16


def split(x):
    high = x.astype(BF16)
    return high, (x - high.astype(F32)).astype(BF16)


def pair_kernel(groups, rows, xi_ref, xj_ref, v_ref, w_ref, proj_ref, fold_ref, pairs_ref, t0_ref, t1_ref, msg_ref):
    width = v_ref.shape[1]
    w_high, w_low = split(w_ref[...])
    acc = jnp.zeros((rows, width), F32)
    total = jnp.zeros((1, width), F32)
    for start in range(0, groups, CHUNK):
        for k in range(start, start + CHUNK):
            dx = xi_ref[0, :, 0:1] - xj_ref[0, k, 0:1, :]
            dy = xi_ref[0, :, 1:2] - xj_ref[0, k, 1:2, :]
            dz = xi_ref[0, :, 2:3] - xj_ref[0, k, 2:3, :]
            dist = jnp.sqrt(dx * dx + dy * dy + dz * dz + 1.0)
            pre = dx * v_ref[0:1, :] + dy * v_ref[1:2, :] + dz * v_ref[2:3, :] + dist * v_ref[3:4, :]
            pairs_ref[0, k] = jnp.tanh(pre)
        flat = pairs_ref[0, start : start + CHUNK].reshape(CHUNK * rows, width)
        high, low = split(flat)
        z = jnp.dot(high, w_high, preferred_element_type=F32)
        z = z + jnp.dot(low, w_high, preferred_element_type=F32)
        z = z + jnp.dot(high, w_low, preferred_element_type=F32)
        t = jnp.tanh(z)
        t0_ref[0, start : start + CHUNK] = t[:, :width].reshape(CHUNK, rows, width)
        t1_ref[0, start : start + CHUNK] = t[:, width:].reshape(CHUNK, rows, width)
        for k in range(start, start + CHUNK):
            row = proj_ref[0, k]
            acc = acc + t0_ref[0, k] * row
            total = total + row
    msg_ref[0] = jnp.dot(acc + total, fold_ref[...], precision=HI, preferred_element_type=F32)


def message_kernel(groups, rows, t_ref, proj_ref, fold_ref, msg_ref):
    width = t_ref.shape[3]
    acc = jnp.zeros((rows, width), F32)
    total = jnp.zeros((1, width), F32)
    for k in range(groups):
        row = proj_ref[0, k]
        acc = acc + t_ref[0, k] * row
        total = total + row
    msg_ref[0] = jnp.dot(acc + total, fold_ref[...], precision=HI, preferred_element_type=F32)


def back_kernel(groups, rows, pairs_ref, t_ref, proj_ref, dm_ref, dproj_ref, gate_ref, tiled_ref, dz_ref):
    width = t_ref.shape[3]

    @pl.when(pl.program_id(0) == 0)
    def _():
        gate_ref[...] = jnp.zeros_like(gate_ref)

    tiled_ref[...] = jnp.concatenate([dm_ref[0]] * PACK, axis=1)
    dims = (((0,), (0,)), ((), ()))
    for start in range(0, groups, CHUNK):
        for k in range(start, start + CHUNK):
            t = t_ref[0, k]
            both = tiled_ref[...] * (1.0 + t)
            dproj_ref[0, k] = jnp.sum(both, axis=0, keepdims=True)
            dz_ref[k - start] = both * (1.0 - t) * proj_ref[0, k]
        p_high, p_low = split(pairs_ref[0, start : start + CHUNK].reshape(CHUNK * rows, width))
        d_high, d_low = split(dz_ref[...].reshape(CHUNK * rows, width))
        part = lax.dot_general(p_high, d_high, dims, preferred_element_type=F32)
        part = part + lax.dot_general(p_low, d_high, dims, preferred_element_type=F32)
        part = part + lax.dot_general(p_high, d_low, dims, preferred_element_type=F32)
        gate_ref[...] += part


def swap(x, axis, bit):
    size = lax.axis_size(axis)
    return lax.ppermute(x, axis, [(i, i ^ bit) for i in range(size)])


def bits_of(axis):
    return [1 << k for k in range(lax.axis_size(axis).bit_length() - 1)]


def sum_over(x, axis):
    for bit in bits_of(axis):
        x = x + swap(x, axis, bit)
    return x


def sum_scatter(x, axis):
    me = lax.axis_index(axis)
    for bit in bits_of(axis):
        mine = (me // bit) % 2
        x = x.reshape((x.shape[0] // 2, 2) + x.shape[1:])
        keep = lax.dynamic_index_in_dim(x, mine, 1, keepdims=False)
        send = lax.dynamic_index_in_dim(x, 1 - mine, 1, keepdims=False)
        x = keep + swap(send, axis, bit)
    return x


def gather(x, axis):
    me = lax.axis_index(axis)
    for bit in reversed(bits_of(axis)):
        first = (me // bit) % 2 == 0
        other = swap(x, axis, bit)
        pair = jnp.stack([jnp.where(first, x, other), jnp.where(first, other, x)], axis=1)
        x = pair.reshape((pair.shape[0] * 2,) + x.shape[1:])
    return x


def whole(shape):
    return pl.BlockSpec(shape, lambda w: (0,) * len(shape))


def per_walker(shape):
    return pl.BlockSpec((1,) + shape, lambda w: (w,) + (0,) * len(shape))


PARAMS = pltpu.CompilerParams(vmem_limit_bytes=50 * 1024 * 1024)


def on_device(positions, targets, w_in, v_in, w_up, w_gate, w_mix, w_msg, bias, w_head):
    walk_size = lax.axis_size("walk")
    elec_size = lax.axis_size("elec")
    own, _, mine = positions.shape
    walkers = own * walk_size
    every = mine * elec_size
    features = v_in.shape[1]
    width = PACK * features
    groups = every // PACK
    rows = -(-mine // 8) * 8

    pos_all = jnp.moveaxis(gather(positions[None], "elec"), 0, 2).reshape(own, 3, every)
    me = lax.axis_index("elec")

    feats = jnp.concatenate(
        [pos_all, jnp.sqrt(jnp.sum(pos_all * pos_all, axis=1, keepdims=True) + 1.0)], axis=1
    )
    states_all = jnp.tanh(jnp.einsum("wci,ch->wih", feats, w_in, precision=HI))
    proj = jnp.einsum("wjh,hp->wjp", states_all, w_up[0], precision=HI)
    own_feats = lax.dynamic_slice_in_dim(feats, me * mine, mine, 2)
    states0 = lax.dynamic_slice_in_dim(states_all, me * mine, mine, 1)

    xi = jnp.pad(jnp.transpose(positions, (0, 2, 1)), ((0, 0), (0, rows - mine), (0, 0)))
    xj = jnp.transpose(pos_all.reshape(own, 3, groups, PACK), (0, 2, 1, 3))
    xj = jnp.repeat(xj, features, axis=3)
    v_tiled = jnp.tile(v_in, (1, PACK))
    eye = jnp.eye(PACK, dtype=F32)
    blocks = [
        (0.5 * eye[:, None, :, None] * w_gate[l][None, :, None, :]).reshape(width, width)
        for l in range(LAYERS)
    ]
    w_pair = jnp.concatenate(blocks, axis=1)
    fold = jnp.tile(jnp.eye(features, dtype=F32), (PACK, 1)) * (0.5 / every)

    big = jax.ShapeDtypeStruct((own, groups, rows, width), F32)
    small = jax.ShapeDtypeStruct((own, rows, features), F32)
    big_spec = per_walker((groups, rows, width))
    row_spec = per_walker((groups, 1, width))
    small_spec = per_walker((rows, features))

    def as_rows(p):
        return p.reshape(own, groups, 1, width)

    rows0 = as_rows(proj)
    pairs, t0, t1, msg = pl.pallas_call(
        functools.partial(pair_kernel, groups, rows),
        grid=(own,),
        out_shape=(big, big, big, small),
        in_specs=[
            per_walker((rows, 3)),
            per_walker((groups, 3, width)),
            whole((4, width)),
            whole((width, LAYERS * width)),
            row_spec,
            whole((width, features)),
        ],
        out_specs=(big_spec, big_spec, big_spec, small_spec),
        compiler_params=PARAMS,
    )(xi, xj, v_tiled, w_pair, rows0, fold)

    def update(h, message, layer):
        pre = jnp.einsum("wih,hk->wik", h, w_mix[layer], precision=HI)
        pre = pre + jnp.einsum("wiq,qk->wik", message, w_msg[layer], precision=HI) + bias[layer]
        return jnp.tanh(pre)

    msg0 = msg[:, :mine]
    act0 = update(states0, msg0, 0)
    states1 = act0 + states0
    local_proj = jnp.einsum("wjh,hp->wjp", states1, w_up[1], precision=HI)
    rows1 = as_rows(jnp.moveaxis(gather(local_proj[None], "elec"), 0, 1))
    msg = pl.pallas_call(
        functools.partial(message_kernel, groups, rows),
        grid=(own,),
        out_shape=small,
        in_specs=[big_spec, row_spec, whole((width, features))],
        out_specs=small_spec,
        compiler_params=PARAMS,
    )(t1, rows1, fold)
    msg1 = msg[:, :mine]
    act1 = update(states1, msg1, 1)
    states2 = act1 + states1

    last = states2.reshape(-1, states2.shape[2]).astype(BF16)
    orbitals = jnp.dot(last, w_head, preferred_element_type=F32)
    flat_targets = targets.reshape(-1, targets.shape[2]).astype(F32)
    d_orb = (2.0 / walkers * (orbitals - flat_targets)).astype(BF16)
    d_states = lax.dot_general(d_orb, w_head, (((1,), (1,)), ((), ())), preferred_element_type=F32)
    d_states = d_states.reshape(states2.shape)
    head = lax.dot_general(d_orb, last, (((0,), (0,)), ((), ())), preferred_element_type=F32)
    head_part = sum_scatter(head.reshape(walk_size, -1, head.shape[1]), "walk")[0]

    def back(d_out, h, act, message, t, rows_l, layer):
        d_pre = d_out * (1.0 - act * act)
        g_bias = jnp.sum(d_pre, axis=(0, 1))
        g_mix = jnp.einsum("wih,wik->hk", h, d_pre, precision=HI)
        g_msg = jnp.einsum("wiq,wik->qk", message, d_pre, precision=HI)
        d_msg = jnp.einsum("wik,qk->wiq", d_pre, w_msg[layer], precision=HI) * (0.5 / every)
        d_msg = jnp.pad(d_msg, ((0, 0), (0, rows - mine), (0, 0)))
        d_rows, g_wide = pl.pallas_call(
            functools.partial(back_kernel, groups, rows),
            grid=(own,),
            out_shape=(
                jax.ShapeDtypeStruct((own, groups, 1, width), F32),
                jax.ShapeDtypeStruct((width, width), F32),
            ),
            in_specs=[big_spec, big_spec, row_spec, small_spec],
            out_specs=(row_spec, whole((width, width))),
            scratch_shapes=[pltpu.VMEM((rows, width), F32), pltpu.VMEM((CHUNK, rows, width), F32)],
            compiler_params=PARAMS,
        )(pairs, t, rows_l, d_msg)
        g_gate = 0.5 * sum(
            g_wide[k * features : (k + 1) * features, k * features : (k + 1) * features]
            for k in range(PACK)
        )
        d_proj = d_rows.reshape(own, elec_size, mine, features)
        d_own = sum_scatter(jnp.moveaxis(d_proj, 1, 0), "elec")[0]
        g_up = jnp.einsum("wjh,wjp->hp", h, d_own, precision=HI)
        d_in = d_out + jnp.einsum("wik,hk->wih", d_pre, w_mix[layer], precision=HI)
        d_in = d_in + jnp.einsum("wjp,hp->wjh", d_own, w_up[layer], precision=HI)
        return d_in, g_up, g_gate, g_mix, g_msg, g_bias

    d1, *g1 = back(d_states, states1, act1, msg1, t1, rows1, 1)
    d0, *g0 = back(d1, states0, act0, msg0, t0, rows0, 0)
    g_in = jnp.einsum("wci,wih->ch", own_feats, d0 * (1.0 - states0 * states0), precision=HI)
    return finish(head_part, g_in, *[jnp.stack([a, b]) for a, b in zip(g0, g1)])


def finish(head_part, *grads):
    size = lax.axis_size("walk")
    width = grads[0].shape[-1]
    flat = jnp.concatenate([g.reshape(-1, width) for g in grads])
    count = flat.shape[0]
    block = -(-count // (8 * size)) * 8
    flat = jnp.pad(flat, ((0, block * size - count), (0, 0))).reshape(size, block, width)
    flat = gather(sum_over(sum_scatter(flat, "walk"), "elec"), "walk").reshape(-1, width)
    outs = []
    start = 0
    for g in grads:
        rows = g.size // width
        outs.append(flat[start : start + rows].reshape(g.shape))
        start += rows
    return (sum_over(head_part, "elec"),) + tuple(outs)


def solution(mesh):
    return jax.shard_map(
        on_device,
        mesh=mesh,
        in_specs=(P("walk", None, "elec"), P("walk", "elec", None)) + (P(),) * 8,
        out_specs=(P("walk", None),) + (P(),) * 6,
        check_vma=False,
    )
```
